512 devices in a mesh: gx: 16 (over y, z_hi), gy: 32 (over z_lo, x, core).
Axes of the slice: x: 4, y: 8, z: 8 (z_hi: 2, z_lo: 4; z = z_hi * 4 + z_lo), core: 2. Of those that a mesh axis runs over, the one named last changes fastest.
Arguments:
- tokens: bfloat16 [2, 192, 12288], P(None, None, 'gx'), may hold values from -6 to 6
- gate_weight: bfloat16 [26624, 12288], P('gy', 'gx'), may hold values from -0.0546875 to 0.0546875
- up_weight: bfloat16 [26624, 12288], P('gy', 'gx'), may hold values from -0.0546875 to 0.0546875
- down_weight: bfloat16 [26624, 12288], P('gy', 'gx'), may hold values from -0.0390625 to 0.0390625
Outputs:
- mixed_out: bfloat16 [2, 192, 12288], P(None, None, 'gx')
The draws below stay inside these ranges and needn't reach their ends.
All inputs are finite; a program needn't handle non-finite values.
Results may differ from the reference program's by a relative error of at most 0.0051.
Values may be sent and summed in bfloat16 or wider, within the bound.
No kernel may reach another device: no remote copies, remote signals or barrier semaphores. Data moves between devices by JAX's collectives and lax.ppermute only.
A program may use at most 64 MiB of HBM per device.

```python
import jax
import jax.numpy as jnp
from jax import lax

D = 12288
FF = 26624
BATCH = 192
STEPS = 2


def block_scale(stream_key, extent, cuts, low, largest):
    gain = 1.0
    for axis_at, blocks in cuts:
        draws = jax.random.uniform(jax.random.fold_in(jax.random.fold_in(stream_key, 6), axis_at), (blocks,), jnp.float32, low / len(cuts), largest / len(cuts))
        gain = gain * jnp.repeat(jnp.exp(draws), extent[axis_at] // blocks).reshape((-1,) + (1,) * (len(extent) - 1 - axis_at))
    return gain


def centred(key, extent, spread, bound, cuts=(), dtype=jnp.bfloat16):
    drawn = spread * jax.random.normal(key, extent, jnp.float32)
    if cuts:
        drawn = drawn * block_scale(key, extent, cuts, -0.22, 0.18)
    return jnp.clip(drawn, -bound, bound).astype(dtype)


def setup_inputs(seed: int = 0) -> dict:
    seeds = jax.random.split(jax.random.key(seed), 5)
    return {
        "tokens": centred(seeds[0], (STEPS, BATCH, D), 1.0, 6.0, ((2, 16),)),
        "gate_weight": centred(seeds[1], (FF, D), D ** -0.5, 0.0546875, ((0, 32), (1, 16))),
        "up_weight": centred(seeds[2], (FF, D), D ** -0.5, 0.0546875, ((0, 32), (1, 16))),
        "down_weight": centred(seeds[3], (FF, D), FF ** -0.5, 0.0390625, ((0, 32), (1, 16))),
    }


def reference(tokens, gate_weight, up_weight, down_weight):
    flat_rows = tokens.reshape(STEPS * BATCH, D)
    dims = (((1,), (1,)), ((), ()))
    gate_total = lax.dot_general(flat_rows, gate_weight, dims, preferred_element_type=jnp.float32)
    up_total = lax.dot_general(flat_rows, up_weight, dims, preferred_element_type=jnp.float32)
    hidden = (jax.nn.silu(gate_total) * up_total).astype(jnp.bfloat16)
    mixed_out = jnp.dot(hidden, down_weight, preferred_element_type=jnp.float32).astype(jnp.bfloat16)
    return mixed_out.reshape(STEPS, BATCH, D)
```

```python
import jax
import jax.numpy as jnp
from jax import lax
from jax.sharding import Mesh, PartitionSpec as P

GX = ("y", "zh")
PLANE = ("zl", "x")


def project(rows, weight):
    return lax.dot_general(rows, weight, (((1,), (1,)), ((), ())), preferred_element_type=jnp.float32)


def exchange(blocks, axes):
    return lax.all_to_all(blocks, axes, 0, 0, tiled=True)


def total(blocks):
    return jnp.sum(blocks.astype(jnp.float32), axis=0)


def spread(block, axes, count):
    return exchange(jnp.broadcast_to(block[None], (count, *block.shape)), axes)


def body(tokens, gate_weight, up_weight, down_weight):
    steps, batch, width = tokens.shape
    rows = steps * batch
    local_ff = gate_weight.shape[0]
    flat = tokens.reshape(rows, width)
    partial_sums = jnp.concatenate((project(flat, gate_weight), project(flat, up_weight)), axis=1)
    sent = partial_sums.astype(jnp.bfloat16).reshape(16, rows // 16, 2 * local_ff)
    summed = total(exchange(sent, GX))
    share = (jax.nn.silu(summed[:, :local_ff]) * summed[:, local_ff:]).astype(jnp.bfloat16)
    hidden = spread(share, GX, 16).reshape(rows, local_ff)
    partial_out = jnp.dot(hidden, down_weight, preferred_element_type=jnp.float32).astype(jnp.bfloat16)
    half = width // 2
    pair = exchange(jnp.stack((partial_out[:, :half], partial_out[:, half:])), "c")
    chip_sum = total(pair).astype(jnp.bfloat16).reshape(16, rows // 16, half)
    out_share = total(exchange(chip_sum, PLANE)).astype(jnp.bfloat16)
    out_half = spread(out_share, PLANE, 16).reshape(rows, half)
    out = lax.all_gather(out_half, "c", axis=1, tiled=True)
    return out.reshape(steps, batch, width)


def solution(mesh):
    fine = Mesh(mesh.devices.reshape(8, 2, 4, 4, 2), ("y", "zh", "zl", "x", "c"))
    gy = ("zl", "x", "c")
    in_specs = (P(None, None, GX), P(gy, GX), P(gy, GX), P(gy, GX))
    return jax.shard_map(body, mesh=fine, in_specs=in_specs, out_specs=P(None, None, GX), check_vma=False)
```

```python
import jax
import jax.numpy as jnp
from jax import lax
from jax.sharding import Mesh, PartitionSpec as P

PLANE = ("zl", "x")
SPLIT = 448


def project(rows, weight):
    return lax.dot_general(rows, weight, (((1,), (1,)), ((), ())), preferred_element_type=jnp.float32)


def pair(rows, gate_weight, up_weight):
    return jnp.concatenate((project(rows, gate_weight), project(rows, up_weight)), axis=1)


def exchange(blocks, axes):
    return lax.all_to_all(blocks, axes, 0, 0, tiled=True)


def spread(block, axes, count):
    return exchange(jnp.broadcast_to(block[None], (count, *block.shape)), axes)


def swap(block):
    return lax.ppermute(block, "zh", [(0, 1), (1, 0)])


def total(blocks):
    return jnp.sum(blocks.astype(jnp.float32), axis=0)


def activate(sums):
    units = sums.shape[-1] // 2
    return (jax.nn.silu(sums[..., :units]) * sums[..., units:]).astype(jnp.bfloat16)


def body(tokens, gate_weight, up_weight, down_weight):
    steps, batch, width = tokens.shape
    rows = steps * batch
    flat = tokens.reshape(rows, width)
    low = lax.axis_index("zh") == 0

    def mine(blocks):
        return jnp.where(low, blocks[0], blocks[1])

    def other(blocks):
        return jnp.where(low, blocks[1], blocks[0])

    def both(own, far):
        return jnp.where(low, jnp.stack((own, far)), jnp.stack((far, own)))

    q = pair(flat, gate_weight[SPLIT:], up_weight[SPLIT:]).reshape(2, rows // 2, -1)
    q_far = swap(other(q).astype(jnp.bfloat16))
    p = pair(flat, gate_weight[:SPLIT], up_weight[:SPLIT]).astype(jnp.bfloat16)
    p_blocks = exchange(p.reshape(8, rows // 8, -1), "y")
    q_half = (mine(q) + q_far.astype(jnp.float32)).astype(jnp.bfloat16)
    q_blocks = exchange(q_half.reshape(8, rows // 16, -1), "y")
    p_sum = total(p_blocks).reshape(2, rows // 16, -1)
    p_far = swap(other(p_sum).astype(jnp.bfloat16))
    q_hidden = activate(total(q_blocks))
    p_hidden = activate(mine(p_sum) + p_far.astype(jnp.float32))

    q_half = spread(q_hidden, "y", 8).reshape(rows // 2, -1)
    p_pair = both(p_hidden, swap(p_hidden)).reshape(rows // 8, -1)
    p_all = spread(p_pair, "y", 8).reshape(rows, -1)
    q_all = both(q_half, swap(q_half)).reshape(rows, -1)
    partial_out = jnp.dot(q_all, down_weight[SPLIT:], preferred_element_type=jnp.float32) + jnp.dot(
        p_all, down_weight[:SPLIT], preferred_element_type=jnp.float32
    )

    half = width // 2
    chip = total(exchange(jnp.stack((partial_out[:, :half], partial_out[:, half:])), "c"))
    chip = chip.astype(jnp.bfloat16).reshape(16, rows // 16, half)
    out_share = total(exchange(chip, PLANE)).astype(jnp.bfloat16)
    out_half = spread(out_share, PLANE, 16).reshape(rows, half)
    out = lax.all_gather(out_half, "c", axis=1, tiled=True)
    return out.reshape(steps, batch, width)


def solution(mesh):
    fine = Mesh(mesh.devices.reshape(8, 2, 4, 4, 2), ("y", "zh", "zl", "x", "c"))
    gx, gy = ("y", "zh"), ("zl", "x", "c")
    in_specs = (P(None, None, gx), P(gy, gx), P(gy, gx), P(gy, gx))
    return jax.shard_map(body, mesh=fine, in_specs=in_specs, out_specs=P(None, None, gx), check_vma=False)
```

```python
import jax
import jax.numpy as jnp
from jax import lax
from jax.sharding import Mesh, PartitionSpec as P

PLANE = ("zl", "x")


def project(rows, weight):
    return lax.dot_general(rows, weight, (((1,), (1,)), ((), ())), preferred_element_type=jnp.float32)


def exchange(blocks, axes):
    return lax.all_to_all(blocks, axes, 0, 0, tiled=True)


def spread(block, axes, count):
    return exchange(jnp.broadcast_to(block[None], (count, *block.shape)), axes)


def total(blocks):
    return jnp.sum(blocks.astype(jnp.float32), axis=0)


def shift(block, step):
    return lax.ppermute(block, "y", [(i, (i + step) % 8) for i in range(8)])


def shift_by_core(block, step):
    pairs = []
    for i in range(8):
        pairs.append((2 * i, 2 * ((i + step) % 8)))
        pairs.append((2 * i + 1, 2 * ((i - step) % 8) + 1))
    return lax.ppermute(block, ("y", "c"), pairs)


def scatter_sum(parts):
    sent = [part.astype(jnp.bfloat16) for part in parts]
    first_core = lax.axis_index("c") == 0
    far = shift_by_core(sent[4], 2).astype(jnp.float32)
    up = shift(jnp.stack((sent[1], sent[3])), 1).astype(jnp.float32)
    down = shift(jnp.stack((sent[7], sent[5])), -1).astype(jnp.float32)
    zero = jnp.zeros((), jnp.float32)
    up_two = parts[2] + up[1] + jnp.where(first_core, far, zero)
    down_two = parts[6] + down[1] + jnp.where(first_core, zero, far)
    last_up = shift(up_two.astype(jnp.bfloat16), 2)
    last_down = shift(down_two.astype(jnp.bfloat16), -2)
    return parts[0] + up[0] + down[0] + last_up.astype(jnp.float32) + last_down.astype(jnp.float32)


def body(tokens, gate_weight, up_weight, down_weight):
    steps, batch, width = tokens.shape
    rows = steps * batch
    local_ff = gate_weight.shape[0]
    flat = tokens.reshape(rows, width)
    turned = lax.dynamic_slice_in_dim(
        jnp.concatenate((flat, flat)), lax.axis_index("y") * (rows // 8), rows, 0
    )
    partial_sums = jnp.concatenate((project(turned, gate_weight), project(turned, up_weight)), axis=1)
    y_sum = scatter_sum(partial_sums.reshape(8, rows // 8, 2 * local_ff))
    near = y_sum.astype(jnp.bfloat16)
    halves = total(lax.all_gather(near, "zh", axis=0))
    summed = halves + (y_sum - near.astype(jnp.float32))
    share = (jax.nn.silu(summed[:, :local_ff]) * summed[:, local_ff:]).astype(jnp.bfloat16)
    hidden = spread(share, "y", 8).reshape(rows, local_ff)
    partial_out = jnp.dot(hidden, down_weight, preferred_element_type=jnp.float32)

    half = width // 2
    first_core = lax.axis_index("c") == 0
    own = jnp.where(first_core, partial_out[:, :half], partial_out[:, half:])
    give = jnp.where(first_core, partial_out[:, half:], partial_out[:, :half]).astype(jnp.bfloat16)
    given = lax.all_gather(give, "c", axis=0)
    chip = own + jnp.where(first_core, given[1], given[0]).astype(jnp.float32)
    chip = chip.astype(jnp.bfloat16).reshape(16, rows // 16, half)
    out_share = total(exchange(chip, PLANE)).astype(jnp.bfloat16)
    out_half = spread(out_share, PLANE, 16).reshape(rows, half)
    out = lax.all_gather(out_half, "c", axis=1, tiled=True)
    return out.reshape(steps, batch, width)


def solution(mesh):
    fine = Mesh(mesh.devices.reshape(8, 2, 4, 4, 2), ("y", "zh", "zl", "x", "c"))
    gx, gy = ("y", "zh"), ("zl", "x", "c")
    in_specs = (P(None, None, gx), P(gy, gx), P(gy, gx), P(gy, gx))
    return jax.shard_map(body, mesh=fine, in_specs=in_specs, out_specs=P(None, None, gx), check_vma=False)
```

```python
import jax
import jax.numpy as jnp
from jax import lax
from jax.experimental import pallas as pl
from jax.experimental.pallas import tpu as pltpu
from jax.sharding import Mesh, PartitionSpec as P

PLANE = ("zl", "x")


ORDER = (4, 1, 3, 7, 5, 0, 2, 6)


def front_kernel(place, tokens, gate, up, far, ups, downs, keep, rows_in, weights, row_sems, weight_sems):
    chunk = rows_in.shape[0] // 8
    units = gate.shape[0]
    cut = units // 2
    loads = []
    for at, (source, start) in enumerate(((gate, 0), (gate, cut), (up, 0), (up, cut))):
        base = 0 if source is gate else units
        loads.append(
            pltpu.make_async_copy(
                source.at[pl.ds(start, cut)], weights.at[pl.ds(base + start, cut)], weight_sems.at[at]
            )
        )
    row_loads = []
    for at, ahead in enumerate(ORDER):
        row = lax.rem(place[0] + ahead, 8) * chunk
        row_loads.append(
            pltpu.make_async_copy(
                tokens.at[pl.ds(pl.multiple_of(row, chunk), chunk)],
                rows_in.at[pl.ds(at * chunk, chunk)],
                row_sems.at[at],
            )
        )
    loads[0].start()
    for load in row_loads:
        load.start()
    for load in loads[1:]:
        load.start()
    for load in row_loads:
        load.wait()
    ready = 0
    for start, stop, needs in ((0, 384, 1), (384, 768, 2), (768, 1152, 3), (1152, 1664, 4)):
        while ready < needs:
            loads[ready].wait()
            ready += 1
        out = lax.dot_general(
            rows_in[...],
            weights[start:stop, :],
            (((1,), (1,)), ((), ())),
            preferred_element_type=jnp.float32,
        )
        sent = out[: 5 * chunk].astype(jnp.bfloat16)
        far[:, start:stop] = sent[:chunk]
        for at in range(2):
            ups[at, :, start:stop] = sent[(1 + at) * chunk : (2 + at) * chunk]
            downs[at, :, start:stop] = sent[(3 + at) * chunk : (4 + at) * chunk]
        for at in range(3):
            keep[at, :, start:stop] = out[(5 + at) * chunk : (6 + at) * chunk]


def front(flat, gate_weight, up_weight):
    rows, width = flat.shape
    units = 2 * gate_weight.shape[0]
    chunk = rows // 8
    place = lax.axis_index("y").astype(jnp.int32).reshape(1)
    whole = pl.BlockSpec(memory_space=pl.ANY)
    vmem = pl.BlockSpec(memory_space=pltpu.VMEM)
    return pl.pallas_call(
        front_kernel,
        out_shape=(
            jax.ShapeDtypeStruct((chunk, units), jnp.bfloat16),
            jax.ShapeDtypeStruct((2, chunk, units), jnp.bfloat16),
            jax.ShapeDtypeStruct((2, chunk, units), jnp.bfloat16),
            jax.ShapeDtypeStruct((3, chunk, units), jnp.float32),
        ),
        in_specs=[pl.BlockSpec(memory_space=pltpu.SMEM), whole, whole, whole],
        out_specs=(vmem, vmem, vmem, vmem),
        scratch_shapes=[
            pltpu.VMEM((rows, width), jnp.bfloat16),
            pltpu.VMEM((units, width), jnp.bfloat16),
            pltpu.SemaphoreType.DMA((8,)),
            pltpu.SemaphoreType.DMA((4,)),
        ],
        compiler_params=pltpu.CompilerParams(vmem_limit_bytes=32 * 1024 * 1024),
        cost_estimate=pl.CostEstimate(
            flops=2 * rows * width * units, bytes_accessed=2 * width * (rows + units), transcendentals=0
        ),
    )(place, flat, gate_weight, up_weight)


def exchange(blocks, axes):
    return lax.all_to_all(blocks, axes, 0, 0, tiled=True)


def spread(block, axes, count):
    return exchange(jnp.broadcast_to(block[None], (count, *block.shape)), axes)


def total(blocks):
    return jnp.sum(blocks.astype(jnp.float32), axis=0)


def shift(block, step):
    return lax.ppermute(block, "y", [(i, (i + step) % 8) for i in range(8)])


def shift_by_core(block, step):
    pairs = []
    for i in range(8):
        pairs.append((2 * i, 2 * ((i + step) % 8)))
        pairs.append((2 * i + 1, 2 * ((i - step) % 8) + 1))
    return lax.ppermute(block, ("y", "c"), pairs)


def scatter_sum(far, ups, downs, keep):
    wide = jnp.float32
    first_core = lax.axis_index("c") == 0
    far = shift_by_core(far, 2)
    up = shift(ups, 1)
    down = shift(downs, -1)
    zero = jnp.zeros((), wide)
    up_two = keep[1] + up[1].astype(wide) + jnp.where(first_core, far.astype(wide), zero)
    down_two = keep[2] + down[1].astype(wide) + jnp.where(first_core, zero, far.astype(wide))
    last_up = shift(up_two.astype(jnp.bfloat16), 2)
    last_down = shift(down_two.astype(jnp.bfloat16), -2)
    return keep[0] + up[0].astype(wide) + down[0].astype(wide) + last_up.astype(wide) + last_down.astype(wide)


def body(tokens, gate_weight, up_weight, down_weight):
    steps, batch, width = tokens.shape
    rows = steps * batch
    local_ff = gate_weight.shape[0]
    flat = tokens.reshape(rows, width)
    y_sum = scatter_sum(*front(flat, gate_weight, up_weight))
    near = y_sum.astype(jnp.bfloat16)
    halves = total(lax.all_gather(near, "zh", axis=0))
    summed = halves + (y_sum - near.astype(jnp.float32))
    share = (jax.nn.silu(summed[:, :local_ff]) * summed[:, local_ff:]).astype(jnp.bfloat16)
    hidden = spread(share, "y", 8).reshape(rows, local_ff)
    partial_out = jnp.dot(hidden, down_weight, preferred_element_type=jnp.float32)

    half = width // 2
    first_core = lax.axis_index("c") == 0
    own = jnp.where(first_core, partial_out[:, :half], partial_out[:, half:])
    give = jnp.where(first_core, partial_out[:, half:], partial_out[:, :half])
    given = lax.all_gather(give, "c", axis=0)
    chip = own + jnp.where(first_core, given[1], given[0])
    chip = chip.astype(jnp.bfloat16).reshape(16, rows // 16, half)
    out_share = total(exchange(chip, PLANE)).astype(jnp.bfloat16)
    out_half = spread(out_share, PLANE, 16).reshape(rows, half)
    out = lax.all_gather(out_half, "c", axis=1, tiled=True)
    return out.reshape(steps, batch, width)


def solution(mesh):
    fine = Mesh(mesh.devices.reshape(8, 2, 4, 4, 2), ("y", "zh", "zl", "x", "c"))
    gx, gy = ("y", "zh"), ("zl", "x", "c")
    in_specs = (P(None, None, gx), P(gy, gx), P(gy, gx), P(gy, gx))
    return jax.shard_map(body, mesh=fine, in_specs=in_specs, out_specs=P(None, None, gx), check_vma=False)
```

```python
import jax
import jax.numpy as jnp
from jax import lax
from jax.experimental import pallas as pl
from jax.experimental.pallas import tpu as pltpu
from jax.sharding import Mesh, PartitionSpec as P

PLANE = ("zl", "x")


ORDER = (4, 1, 3, 7, 5, 0, 2, 6)


def front_kernel(place, tokens, gate, up, far, ups, downs, keep, rows_in, weights, row_sems, weight_sems):
    chunk = rows_in.shape[0] // 8
    units = gate.shape[0]
    cut = units // 2
    loads = []
    for at, (source, start) in enumerate(((gate, 0), (gate, cut), (up, 0), (up, cut))):
        base = 0 if source is gate else units
        loads.append(
            pltpu.make_async_copy(
                source.at[pl.ds(start, cut)], weights.at[pl.ds(base + start, cut)], weight_sems.at[at]
            )
        )
    row_loads = []
    for at, ahead in enumerate(ORDER):
        row = lax.rem(place[0] + ahead, 8) * chunk
        row_loads.append(
            pltpu.make_async_copy(
                tokens.at[pl.ds(pl.multiple_of(row, chunk), chunk)],
                rows_in.at[pl.ds(at * chunk, chunk)],
                row_sems.at[at],
            )
        )
    loads[0].start()
    for load in row_loads:
        load.start()
    for load in loads[1:]:
        load.start()
    for load in row_loads:
        load.wait()
    ready = 0
    for start, stop, needs in ((0, 384, 1), (384, 768, 2), (768, 1152, 3), (1152, 1664, 4)):
        while ready < needs:
            loads[ready].wait()
            ready += 1
        out = lax.dot_general(
            rows_in[...],
            weights[start:stop, :],
            (((1,), (1,)), ((), ())),
            preferred_element_type=jnp.float32,
        )
        sent = out[: 5 * chunk].astype(jnp.bfloat16)
        far[:, start:stop] = sent[:chunk]
        for at in range(2):
            ups[at, :, start:stop] = sent[(1 + at) * chunk : (2 + at) * chunk]
            downs[at, :, start:stop] = sent[(3 + at) * chunk : (4 + at) * chunk]
        for at in range(3):
            keep[at, :, start:stop] = out[(5 + at) * chunk : (6 + at) * chunk]


def front(flat, gate_weight, up_weight):
    rows, width = flat.shape
    units = 2 * gate_weight.shape[0]
    chunk = rows // 8
    place = lax.axis_index("y").astype(jnp.int32).reshape(1)
    whole = pl.BlockSpec(memory_space=pltpu.HBM)
    vmem = pl.BlockSpec(memory_space=pltpu.VMEM)
    return pl.pallas_call(
        front_kernel,
        out_shape=(
            jax.ShapeDtypeStruct((chunk, units), jnp.bfloat16),
            jax.ShapeDtypeStruct((2, chunk, units), jnp.bfloat16),
            jax.ShapeDtypeStruct((2, chunk, units), jnp.bfloat16),
            jax.ShapeDtypeStruct((3, chunk, units), jnp.float32),
        ),
        in_specs=[pl.BlockSpec(memory_space=pltpu.SMEM), whole, whole, whole],
        out_specs=(vmem, vmem, vmem, vmem),
        scratch_shapes=[
            pltpu.VMEM((rows, width), jnp.bfloat16),
            pltpu.VMEM((units, width), jnp.bfloat16),
            pltpu.SemaphoreType.DMA((8,)),
            pltpu.SemaphoreType.DMA((4,)),
        ],
        compiler_params=pltpu.CompilerParams(vmem_limit_bytes=32 * 1024 * 1024),
        cost_estimate=pl.CostEstimate(
            flops=2 * rows * width * units, bytes_accessed=2 * width * (rows + units), transcendentals=0
        ),
    )(place, flat, gate_weight, up_weight)


def exchange(blocks, axes):
    return lax.all_to_all(blocks, axes, 0, 0, tiled=True)


def spread(block, axes, count):
    return exchange(jnp.broadcast_to(block[None], (count, *block.shape)), axes)


def total(blocks):
    return jnp.sum(blocks.astype(jnp.float32), axis=0)


def shift(block, step):
    return lax.ppermute(block, "y", [(i, (i + step) % 8) for i in range(8)])


def shift_by_core(block, step):
    pairs = []
    for i in range(8):
        pairs.append((2 * i, 2 * ((i + step) % 8)))
        pairs.append((2 * i + 1, 2 * ((i - step) % 8) + 1))
    return lax.ppermute(block, ("y", "c"), pairs)


def small_call(kernel, out_shapes, *operands, smem=0, flops=0):
    vmem = pl.BlockSpec(memory_space=pltpu.VMEM)
    scalar = pl.BlockSpec(memory_space=pltpu.SMEM)
    shapes = [jax.ShapeDtypeStruct(shape, dtype) for shape, dtype in out_shapes]
    moved = sum(x.size * x.dtype.itemsize for x in operands[smem:]) + sum(
        x.size * jnp.dtype(x.dtype).itemsize for x in shapes
    )
    return pl.pallas_call(
        kernel,
        out_shape=shapes,
        in_specs=[scalar] * smem + [vmem] * (len(operands) - smem),
        out_specs=[vmem] * len(shapes),
        compiler_params=pltpu.CompilerParams(vmem_limit_bytes=24 * 1024 * 1024),
        cost_estimate=pl.CostEstimate(flops=flops, bytes_accessed=moved, transcendentals=0),
    )(*operands)


def merge_kernel(core, far, up, down, keep, up_two, down_two, base):
    wide = jnp.float32
    to_up = jnp.where(core[0] == 0, 1.0, 0.0).astype(wide)
    far_rows = far[...].astype(wide)
    up_two[...] = (keep[1] + up[1].astype(wide) + far_rows * to_up).astype(jnp.bfloat16)
    down_two[...] = (keep[2] + down[1].astype(wide) + far_rows * (1.0 - to_up)).astype(jnp.bfloat16)
    base[...] = keep[0] + up[0].astype(wide) + down[0].astype(wide)


def finish_kernel(base, last_up, last_down, near, rest):
    wide = jnp.float32
    y_sum = base[...] + last_up[...].astype(wide) + last_down[...].astype(wide)
    rounded = y_sum.astype(jnp.bfloat16)
    near[...] = rounded
    rest[...] = y_sum - rounded.astype(wide)


def activate_kernel(halves, rest, spread_out):
    wide = jnp.float32
    rows, units = spread_out.shape[1:]
    summed = rest[...] + halves[:rows].astype(wide) + halves[rows:].astype(wide)
    gate = summed[:, :units]
    hidden = (gate / (1.0 + jnp.exp(-gate)) * summed[:, units:]).astype(jnp.bfloat16)
    for at in range(spread_out.shape[0]):
        spread_out[at] = hidden


def down_kernel(hidden, weight, out):
    blocks, rows, units = hidden.shape
    left = hidden[...].reshape(blocks * rows, units)
    half = out.shape[2]
    for at in range(2):
        out[at] = jnp.dot(left, weight[:, at * half : (at + 1) * half], preferred_element_type=jnp.float32)


def scatter_sum(far, ups, downs, keep):
    core = lax.axis_index("c").astype(jnp.int32).reshape(1)
    far = shift_by_core(far, 2)
    up = shift(ups, 1)
    down = shift(downs, -1)
    one = far.shape
    up_two, down_two, base = small_call(
        merge_kernel,
        ((one, jnp.bfloat16), (one, jnp.bfloat16), (one, jnp.float32)),
        core, far, up, down, keep, smem=1,
    )
    last_up = shift(up_two, 2)
    last_down = shift(down_two, -2)
    return small_call(finish_kernel, ((one, jnp.bfloat16), (one, jnp.float32)), base, last_up, last_down)


def body(tokens, gate_weight, up_weight, down_weight):
    steps, batch, width = tokens.shape
    rows = steps * batch
    local_ff = gate_weight.shape[0]
    flat = tokens.reshape(rows, width)
    near, rest = scatter_sum(*front(flat, gate_weight, up_weight))
    halves = lax.all_gather(near, "zh", axis=0, tiled=True)
    blocks = (8, rows // 8, local_ff)
    (shares,) = small_call(activate_kernel, ((blocks, jnp.bfloat16),), halves, rest)
    hidden = exchange(shares, "y")
    half = width // 2
    (partial_out,) = small_call(
        down_kernel,
        (((2, rows, half), jnp.float32),),
        hidden, down_weight, flops=2 * rows * local_ff * width,
    )
    chip = total(exchange(partial_out, "c"))
    chip = chip.astype(jnp.bfloat16).reshape(16, rows // 16, half)
    out_share = total(exchange(chip, PLANE)).astype(jnp.bfloat16)
    out_half = spread(out_share, PLANE, 16).reshape(rows, half)
    out = lax.all_gather(out_half, "c", axis=1, tiled=True)
    return out.reshape(steps, batch, width)


def solution(mesh):
    fine = Mesh(mesh.devices.reshape(8, 2, 4, 4, 2), ("y", "zh", "zl", "x", "c"))
    gx, gy = ("y", "zh"), ("zl", "x", "c")
    in_specs = (P(None, None, gx), P(gy, gx), P(gy, gx), P(gy, gx))
    return jax.shard_map(body, mesh=fine, in_specs=in_specs, out_specs=P(None, None, gx), check_vma=False)
```

```python
import jax
import jax.numpy as jnp
from jax import lax
from jax.experimental import pallas as pl
from jax.experimental.pallas import tpu as pltpu
from jax.sharding import Mesh, PartitionSpec as P

PLANE = ("x", "zl")


SENT = (4, 1, 3, 7, 5)
KEPT = (0, 2, 6)


def blocks_of(order, place, tokens, gate, up, rows_in, weights, row_sems, weight_sems):
    chunk = rows_in.shape[0] // len(order)
    units = gate.shape[0]
    loads = [
        pltpu.make_async_copy(source, weights.at[pl.ds(base, units)], weight_sems.at[at])
        for at, (source, base) in enumerate(((gate, 0), (up, units)))
    ]
    for at, ahead in enumerate(order):
        row = lax.rem(place[0] + ahead, 8) * chunk
        loads.append(
            pltpu.make_async_copy(
                tokens.at[pl.ds(pl.multiple_of(row, chunk), chunk)],
                rows_in.at[pl.ds(at * chunk, chunk)],
                row_sems.at[at],
            )
        )
    for load in loads:
        load.start()
    for load in loads:
        load.wait()
    return lax.dot_general(
        rows_in[...], weights[...], (((1,), (1,)), ((), ())), preferred_element_type=jnp.float32
    )


def send_kernel(place, tokens, gate, up, far, ups, downs, *scratch):
    chunk = far.shape[0]
    sent = blocks_of(SENT, place, tokens, gate, up, *scratch).astype(jnp.bfloat16)
    far[...] = sent[:chunk]
    for at in range(2):
        ups[at] = sent[(1 + at) * chunk : (2 + at) * chunk]
        downs[at] = sent[(3 + at) * chunk : (4 + at) * chunk]


def keep_kernel(place, tokens, gate, up, keep, *scratch):
    chunk = keep.shape[1]
    out = blocks_of(KEPT, place, tokens, gate, up, *scratch)
    for at in range(3):
        keep[at] = out[at * chunk : (at + 1) * chunk]


def front(flat, gate_weight, up_weight):
    rows, width = flat.shape
    units = 2 * gate_weight.shape[0]
    chunk = rows // 8
    place = lax.axis_index("y").astype(jnp.int32).reshape(1)
    whole = pl.BlockSpec(memory_space=pltpu.HBM)
    vmem = pl.BlockSpec(memory_space=pltpu.VMEM)

    def call(kernel, order, out_shapes):
        taken = len(order) * chunk
        return pl.pallas_call(
            kernel,
            out_shape=out_shapes,
            in_specs=[pl.BlockSpec(memory_space=pltpu.SMEM), whole, whole, whole],
            out_specs=[vmem] * len(out_shapes),
            scratch_shapes=[
                pltpu.VMEM((taken, width), jnp.bfloat16),
                pltpu.VMEM((units, width), jnp.bfloat16),
                pltpu.SemaphoreType.DMA((len(order),)),
                pltpu.SemaphoreType.DMA((2,)),
            ],
            compiler_params=pltpu.CompilerParams(vmem_limit_bytes=60 * 1024 * 1024),
            cost_estimate=pl.CostEstimate(
                flops=2 * taken * width * units,
                bytes_accessed=2 * width * (taken + units),
                transcendentals=0,
            ),
        )(place, flat, gate_weight, up_weight)

    one = jax.ShapeDtypeStruct((chunk, units), jnp.bfloat16)
    two = jax.ShapeDtypeStruct((2, chunk, units), jnp.bfloat16)
    far, ups, downs = call(send_kernel, SENT, [one, two, two])
    (keep,) = call(keep_kernel, KEPT, [jax.ShapeDtypeStruct((3, chunk, units), jnp.float32)])
    return far, ups, downs, keep


def exchange(blocks, axes):
    return lax.all_to_all(blocks, axes, 0, 0, tiled=True)


def spread(block, axes, count):
    return exchange(jnp.broadcast_to(block[None], (count, *block.shape)), axes)


def total(blocks):
    return jnp.sum(blocks.astype(jnp.float32), axis=0)


def shift(block, step):
    return lax.ppermute(block, "y", [(i, (i + step) % 8) for i in range(8)])


def shift_by_core(block, step):
    pairs = []
    for i in range(8):
        pairs.append((2 * i, 2 * ((i + step) % 8)))
        pairs.append((2 * i + 1, 2 * ((i - step) % 8) + 1))
    return lax.ppermute(block, ("y", "c"), pairs)


def small_call(kernel, out_shapes, *operands, smem=0, flops=0):
    vmem = pl.BlockSpec(memory_space=pltpu.VMEM)
    scalar = pl.BlockSpec(memory_space=pltpu.SMEM)
    shapes = [jax.ShapeDtypeStruct(shape, dtype) for shape, dtype in out_shapes]
    moved = sum(x.size * x.dtype.itemsize for x in operands[smem:]) + sum(
        x.size * jnp.dtype(x.dtype).itemsize for x in shapes
    )
    return pl.pallas_call(
        kernel,
        out_shape=shapes,
        in_specs=[scalar] * smem + [vmem] * (len(operands) - smem),
        out_specs=[vmem] * len(shapes),
        compiler_params=pltpu.CompilerParams(vmem_limit_bytes=24 * 1024 * 1024),
        cost_estimate=pl.CostEstimate(flops=flops, bytes_accessed=moved, transcendentals=0),
    )(*operands)


def merge_kernel(core, far, up, down, keep, down_two, up_two, base):
    wide = jnp.float32
    to_up = jnp.where(core[0] == 0, 0.0, 1.0).astype(wide)
    far_rows = far[...].astype(wide)
    up_two[...] = (keep[1] + up[1].astype(wide) + far_rows * to_up).astype(jnp.bfloat16)
    down_two[...] = (keep[2] + down[1].astype(wide) + far_rows * (1.0 - to_up)).astype(jnp.bfloat16)
    base[...] = keep[0] + up[0].astype(wide) + down[0].astype(wide)


def finish_kernel(base, last_up, last_down, near, rest):
    wide = jnp.float32
    y_sum = base[...] + last_up[...].astype(wide) + last_down[...].astype(wide)
    rounded = y_sum.astype(jnp.bfloat16)
    near[...] = rounded
    rest[...] = y_sum - rounded.astype(wide)


def activate_kernel(halves, rest, spread_out):
    wide = jnp.float32
    rows, units = spread_out.shape[1:]
    summed = rest[...] + halves[:rows].astype(wide) + halves[rows:].astype(wide)
    gate = summed[:, :units]
    hidden = (gate / (1.0 + jnp.exp(-gate)) * summed[:, units:]).astype(jnp.bfloat16)
    for at in range(spread_out.shape[0]):
        spread_out[at] = hidden


def down_kernel(core, hidden, weight, own, give):
    blocks, rows, units = hidden.shape
    left = hidden[...].reshape(blocks * rows, units)
    half = own.shape[1]
    mine = pl.ds(pl.multiple_of(core[0] * half, half), half)
    other = pl.ds(pl.multiple_of((1 - core[0]) * half, half), half)
    own[...] = jnp.dot(left, weight[:, mine], preferred_element_type=jnp.float32)
    give[...] = jnp.dot(left, weight[:, other], preferred_element_type=jnp.float32).astype(jnp.bfloat16)


def scatter_sum(far, ups, downs, keep):
    core = lax.axis_index("c").astype(jnp.int32).reshape(1)
    far = shift_by_core(far, -2)
    up = shift(ups, 1)
    down = shift(downs, -1)
    one = far.shape
    down_two, up_two, base = small_call(
        merge_kernel,
        ((one, jnp.bfloat16), (one, jnp.bfloat16), (one, jnp.float32)),
        core, far, up, down, keep, smem=1,
    )
    last_down = shift(down_two, -2)
    last_up = shift(up_two, 2)
    return small_call(finish_kernel, ((one, jnp.bfloat16), (one, jnp.float32)), base, last_down, last_up)


def body(tokens, gate_weight, up_weight, down_weight):
    steps, batch, width = tokens.shape
    rows = steps * batch
    local_ff = gate_weight.shape[0]
    flat = tokens.reshape(rows, width)
    near, rest = scatter_sum(*front(flat, gate_weight, up_weight))
    halves = lax.all_gather(near, "zh", axis=0, tiled=True)
    blocks = (8, rows // 8, local_ff)
    (shares,) = small_call(activate_kernel, ((blocks, jnp.bfloat16),), halves, rest)
    core = lax.axis_index("c").astype(jnp.int32)
    shares, core, first = lax.optimization_barrier((shares, core, core == 0))
    hidden = exchange(shares, "y")
    half = width // 2
    own, give = small_call(
        down_kernel,
        (((rows, half), jnp.float32), ((rows, half), jnp.bfloat16)),
        core.reshape(1), hidden, down_weight, smem=1, flops=2 * rows * local_ff * width,
    )
    given = lax.all_gather(give, "c", axis=0)
    chip = own + jnp.where(first, given[1], given[0]).astype(jnp.float32)
    chip = chip.astype(jnp.bfloat16).reshape(16, rows // 16, half)
    out_share = total(exchange(chip, PLANE)).astype(jnp.bfloat16)
    out_half = spread(out_share, PLANE, 16).reshape(rows, half)
    out = lax.all_gather(out_half, "c", axis=1, tiled=True)
    return out.reshape(steps, batch, width)


def solution(mesh):
    fine = Mesh(mesh.devices.reshape(8, 2, 4, 4, 2), ("y", "zh", "zl", "x", "c"))
    gx, gy = ("y", "zh"), ("zl", "x", "c")
    in_specs = (P(None, None, gx), P(gy, gx), P(gy, gx), P(gy, gx))
    return jax.shard_map(body, mesh=fine, in_specs=in_specs, out_specs=P(None, None, gx), check_vma=False)
```

```python
import jax
import jax.numpy as jnp
from jax import lax
from jax.experimental import pallas as pl
from jax.experimental.pallas import tpu as pltpu
from jax.sharding import Mesh, PartitionSpec as P

PLANE = ("x", "zl")


SENT = (4, 1, 3, 7, 5)
KEPT = (0, 2, 6)


def blocks_of(order, place, tokens, gate, up, rows_in, weights, row_sems, weight_sems):
    chunk = rows_in.shape[0] // len(order)
    units = gate.shape[0]
    loads = [
        pltpu.make_async_copy(source, weights.at[pl.ds(base, units)], weight_sems.at[at])
        for at, (source, base) in enumerate(((gate, 0), (up, units)))
    ]
    for at, ahead in enumerate(order):
        row = lax.rem(place[0] + ahead, 8) * chunk
        loads.append(
            pltpu.make_async_copy(
                tokens.at[pl.ds(pl.multiple_of(row, chunk), chunk)],
                rows_in.at[pl.ds(at * chunk, chunk)],
                row_sems.at[at],
            )
        )
    for load in loads:
        load.start()
    for load in loads:
        load.wait()
    return lax.dot_general(
        rows_in[...], weights[...], (((1,), (1,)), ((), ())), preferred_element_type=jnp.float32
    )


def send_kernel(place, tokens, gate, up, far, ups, downs, *scratch):
    chunk = far.shape[0]
    sent = blocks_of(SENT, place, tokens, gate, up, *scratch).astype(jnp.bfloat16)
    far[...] = sent[:chunk]
    for at in range(2):
        ups[at] = sent[(1 + at) * chunk : (2 + at) * chunk]
        downs[at] = sent[(3 + at) * chunk : (4 + at) * chunk]


def keep_kernel(place, tokens, gate, up, keep, own, *scratch):
    chunk = keep.shape[1]
    out = blocks_of(KEPT, place, tokens, gate, up, *scratch)
    own[...] = out[:chunk]
    for at in range(2):
        keep[at] = out[(at + 1) * chunk : (at + 2) * chunk]


def front(flat, gate_weight, up_weight):
    rows, width = flat.shape
    units = 2 * gate_weight.shape[0]
    chunk = rows // 8
    place = lax.axis_index("y").astype(jnp.int32).reshape(1)
    whole = pl.BlockSpec(memory_space=pltpu.HBM)
    vmem = pl.BlockSpec(memory_space=pltpu.VMEM)

    def call(kernel, order, out_shapes):
        taken = len(order) * chunk
        return pl.pallas_call(
            kernel,
            out_shape=out_shapes,
            in_specs=[pl.BlockSpec(memory_space=pltpu.SMEM), whole, whole, whole],
            out_specs=[vmem] * len(out_shapes),
            scratch_shapes=[
                pltpu.VMEM((taken, width), jnp.bfloat16),
                pltpu.VMEM((units, width), jnp.bfloat16),
                pltpu.SemaphoreType.DMA((len(order),)),
                pltpu.SemaphoreType.DMA((2,)),
            ],
            compiler_params=pltpu.CompilerParams(vmem_limit_bytes=60 * 1024 * 1024),
            cost_estimate=pl.CostEstimate(
                flops=2 * taken * width * units,
                bytes_accessed=2 * width * (taken + units),
                transcendentals=0,
            ),
        )(place, flat, gate_weight, up_weight)

    one = jax.ShapeDtypeStruct((chunk, units), jnp.bfloat16)
    two = jax.ShapeDtypeStruct((2, chunk, units), jnp.bfloat16)
    far, ups, downs = call(send_kernel, SENT, [one, two, two])
    kept = jax.ShapeDtypeStruct((2, chunk, units), jnp.float32)
    keep, own = call(keep_kernel, KEPT, [kept, jax.ShapeDtypeStruct((chunk, units), jnp.float32)])
    return far, ups, downs, keep, own


def exchange(blocks, axes):
    return lax.all_to_all(blocks, axes, 0, 0, tiled=True)


def spread(block, axes, count):
    return exchange(jnp.broadcast_to(block[None], (count, *block.shape)), axes)


def total(blocks):
    return jnp.sum(blocks.astype(jnp.float32), axis=0)


def shift(block, step):
    return lax.ppermute(block, "y", [(i, (i + step) % 8) for i in range(8)])


def shift_by_core(block, step):
    pairs = []
    for i in range(8):
        pairs.append((2 * i, 2 * ((i + step) % 8)))
        pairs.append((2 * i + 1, 2 * ((i - step) % 8) + 1))
    return lax.ppermute(block, ("y", "c"), pairs)


def small_call(kernel, out_shapes, *operands, smem=0, flops=0):
    vmem = pl.BlockSpec(memory_space=pltpu.VMEM)
    scalar = pl.BlockSpec(memory_space=pltpu.SMEM)
    shapes = [jax.ShapeDtypeStruct(shape, dtype) for shape, dtype in out_shapes]
    moved = sum(x.size * x.dtype.itemsize for x in operands[smem:]) + sum(
        x.size * jnp.dtype(x.dtype).itemsize for x in shapes
    )
    return pl.pallas_call(
        kernel,
        out_shape=shapes,
        in_specs=[scalar] * smem + [vmem] * (len(operands) - smem),
        out_specs=[vmem] * len(shapes),
        compiler_params=pltpu.CompilerParams(vmem_limit_bytes=24 * 1024 * 1024),
        cost_estimate=pl.CostEstimate(flops=flops, bytes_accessed=moved, transcendentals=0),
    )(*operands)


def merge_kernel(core, far, up, down, keep, down_two, up_two):
    wide = jnp.float32
    to_up = jnp.where(core[0] == 0, 0.0, 1.0).astype(wide)
    far_rows = far[...].astype(wide)
    up_two[...] = (keep[0] + up[1].astype(wide) + far_rows * to_up).astype(jnp.bfloat16)
    down_two[...] = (keep[1] + down[1].astype(wide) + far_rows * (1.0 - to_up)).astype(jnp.bfloat16)


def finish_kernel(own, up, down, last_up, last_down, near, rest):
    wide = jnp.float32
    y_sum = own[...] + up[0].astype(wide) + down[0].astype(wide)
    y_sum = y_sum + last_up[...].astype(wide) + last_down[...].astype(wide)
    rounded = y_sum.astype(jnp.bfloat16)
    near[...] = rounded
    rest[...] = y_sum - rounded.astype(wide)


def activate_kernel(halves, rest, spread_out):
    wide = jnp.float32
    rows, units = spread_out.shape[1:]
    summed = rest[...] + halves[:rows].astype(wide) + halves[rows:].astype(wide)
    gate = summed[:, :units]
    hidden = (gate / (1.0 + jnp.exp(-gate)) * summed[:, units:]).astype(jnp.bfloat16)
    for at in range(spread_out.shape[0]):
        spread_out[at] = hidden


def down_kernel(core, hidden, weight, own, give):
    blocks, rows, units = hidden.shape
    left = hidden[...].reshape(blocks * rows, units)
    half = own.shape[1]
    mine = pl.ds(pl.multiple_of(core[0] * half, half), half)
    other = pl.ds(pl.multiple_of((1 - core[0]) * half, half), half)
    own[...] = jnp.dot(left, weight[:, mine], preferred_element_type=jnp.float32)
    give[...] = jnp.dot(left, weight[:, other], preferred_element_type=jnp.float32).astype(jnp.bfloat16)


def scatter_sum(far, ups, downs, keep, own):
    core = lax.axis_index("c").astype(jnp.int32).reshape(1)
    far = shift_by_core(far, -2)
    up = shift(ups, 1)
    down = shift(downs, -1)
    one = far.shape
    down_two, up_two = small_call(
        merge_kernel,
        ((one, jnp.bfloat16), (one, jnp.bfloat16)),
        core, far, up, down, keep, smem=1,
    )
    last_down = shift(down_two, -2)
    last_up = shift(up_two, 2)
    return small_call(finish_kernel, ((one, jnp.bfloat16), (one, jnp.float32)), own, up, down, last_down, last_up)


def body(tokens, gate_weight, up_weight, down_weight):
    steps, batch, width = tokens.shape
    rows = steps * batch
    local_ff = gate_weight.shape[0]
    flat = tokens.reshape(rows, width)
    near, rest = scatter_sum(*front(flat, gate_weight, up_weight))
    halves = lax.all_gather(near, "zh", axis=0, tiled=True)
    blocks = (8, rows // 8, local_ff)
    (shares,) = small_call(activate_kernel, ((blocks, jnp.bfloat16),), halves, rest)
    core = lax.axis_index("c").astype(jnp.int32)
    shares, core, first = lax.optimization_barrier((shares, core, core == 0))
    hidden = exchange(shares, "y")
    half = width // 2
    own, give = small_call(
        down_kernel,
        (((rows, half), jnp.float32), ((rows, half), jnp.bfloat16)),
        core.reshape(1), hidden, down_weight, smem=1, flops=2 * rows * local_ff * width,
    )
    given = lax.all_gather(give, "c", axis=0)
    chip = own + jnp.where(first, given[1], given[0]).astype(jnp.float32)
    chip = chip.astype(jnp.bfloat16).reshape(16, rows // 16, half)
    out_share = total(exchange(chip, PLANE)).astype(jnp.bfloat16)
    out_half = spread(out_share, PLANE, 16).reshape(rows, half)
    out = lax.all_gather(out_half, "c", axis=1, tiled=True)
    return out.reshape(steps, batch, width)


def solution(mesh):
    fine = Mesh(mesh.devices.reshape(8, 2, 4, 4, 2), ("y", "zh", "zl", "x", "c"))
    gx, gy = ("y", "zh"), ("zl", "x", "c")
    in_specs = (P(None, None, gx), P(gy, gx), P(gy, gx), P(gy, gx))
    return jax.shard_map(body, mesh=fine, in_specs=in_specs, out_specs=P(None, None, gx), check_vma=False)
```

```python
import jax
import jax.numpy as jnp
from jax import lax
from jax.experimental import pallas as pl
from jax.experimental.pallas import tpu as pltpu
from jax.sharding import Mesh, PartitionSpec as P

PLANE = ("x", "zl")


SENT = (4, 1, 3, 7, 5)
KEPT = (0, 2, 6)


def blocks_of(order, place, tokens, gate, up, rows_in, weights, row_sems, weight_sems):
    chunk = rows_in.shape[0] // len(order)
    units = gate.shape[0]
    loads = [
        pltpu.make_async_copy(source, weights.at[pl.ds(base, units)], weight_sems.at[at])
        for at, (source, base) in enumerate(((gate, 0), (up, units)))
    ]
    for at, ahead in enumerate(order):
        row = lax.rem(place[0] + ahead, 8) * chunk
        loads.append(
            pltpu.make_async_copy(
                tokens.at[pl.ds(pl.multiple_of(row, chunk), chunk)],
                rows_in.at[pl.ds(at * chunk, chunk)],
                row_sems.at[at],
            )
        )
    for load in loads:
        load.start()
    for load in loads:
        load.wait()
    return lax.dot_general(
        rows_in[...], weights[...], (((1,), (1,)), ((), ())), preferred_element_type=jnp.float32
    )


def send_kernel(place, tokens, gate, up, far, ups, downs, *scratch):
    chunk = far.shape[0]
    sent = blocks_of(SENT, place, tokens, gate, up, *scratch).astype(jnp.bfloat16)
    far[...] = sent[:chunk]
    for at in range(2):
        ups[at] = sent[(1 + at) * chunk : (2 + at) * chunk]
        downs[at] = sent[(3 + at) * chunk : (4 + at) * chunk]


def keep_kernel(place, tokens, gate, up, keep, own, *scratch):
    chunk = keep.shape[1]
    out = blocks_of(KEPT, place, tokens, gate, up, *scratch)
    own[...] = out[:chunk]
    for at in range(2):
        keep[at] = out[(at + 1) * chunk : (at + 2) * chunk]


def front(flat, gate_weight, up_weight):
    rows, width = flat.shape
    units = 2 * gate_weight.shape[0]
    chunk = rows // 8
    place = lax.axis_index("y").astype(jnp.int32).reshape(1)
    whole = pl.BlockSpec(memory_space=pltpu.HBM)
    vmem = pl.BlockSpec(memory_space=pltpu.VMEM)

    def call(kernel, order, out_shapes):
        taken = len(order) * chunk
        return pl.pallas_call(
            kernel,
            out_shape=out_shapes,
            in_specs=[pl.BlockSpec(memory_space=pltpu.SMEM), whole, whole, whole],
            out_specs=[vmem] * len(out_shapes),
            scratch_shapes=[
                pltpu.VMEM((taken, width), jnp.bfloat16),
                pltpu.VMEM((units, width), jnp.bfloat16),
                pltpu.SemaphoreType.DMA((len(order),)),
                pltpu.SemaphoreType.DMA((2,)),
            ],
            compiler_params=pltpu.CompilerParams(vmem_limit_bytes=60 * 1024 * 1024),
            cost_estimate=pl.CostEstimate(
                flops=2 * taken * width * units,
                bytes_accessed=2 * width * (taken + units),
                transcendentals=0,
            ),
        )(place, flat, gate_weight, up_weight)

    one = jax.ShapeDtypeStruct((chunk, units), jnp.bfloat16)
    two = jax.ShapeDtypeStruct((2, chunk, units), jnp.bfloat16)
    far, ups, downs = call(send_kernel, SENT, [one, two, two])
    kept = jax.ShapeDtypeStruct((2, chunk, units), jnp.float32)
    keep, own = call(keep_kernel, KEPT, [kept, jax.ShapeDtypeStruct((chunk, units), jnp.float32)])
    return far, ups, downs, keep, own


def exchange(blocks, axes):
    return lax.all_to_all(blocks, axes, 0, 0, tiled=True)


def spread(block, axes, count):
    return exchange(jnp.broadcast_to(block[None], (count, *block.shape)), axes)


def total(blocks):
    return jnp.sum(blocks.astype(jnp.float32), axis=0)


def shift(block, step):
    return lax.ppermute(block, "y", [(i, (i + step) % 8) for i in range(8)])


def shift_by_core(block, step):
    pairs = []
    for i in range(8):
        pairs.append((2 * i, 2 * ((i + step) % 8)))
        pairs.append((2 * i + 1, 2 * ((i - step) % 8) + 1))
    return lax.ppermute(block, ("y", "c"), pairs)


def small_call(kernel, out_shapes, *operands, smem=0, flops=0):
    vmem = pl.BlockSpec(memory_space=pltpu.VMEM)
    scalar = pl.BlockSpec(memory_space=pltpu.SMEM)
    shapes = [jax.ShapeDtypeStruct(shape, dtype) for shape, dtype in out_shapes]
    moved = sum(x.size * x.dtype.itemsize for x in operands[smem:]) + sum(
        x.size * jnp.dtype(x.dtype).itemsize for x in shapes
    )
    return pl.pallas_call(
        kernel,
        out_shape=shapes,
        in_specs=[scalar] * smem + [vmem] * (len(operands) - smem),
        out_specs=[vmem] * len(shapes),
        compiler_params=pltpu.CompilerParams(vmem_limit_bytes=24 * 1024 * 1024),
        cost_estimate=pl.CostEstimate(flops=flops, bytes_accessed=moved, transcendentals=0),
    )(*operands)


def merge_kernel(core, far, up, down, keep, down_two, up_two):
    wide = jnp.float32
    to_up = jnp.where(core[0] == 0, 0.0, 1.0).astype(wide)
    far_rows = far[...].astype(wide)
    up_two[...] = (keep[0] + up[1].astype(wide) + far_rows * to_up).astype(jnp.bfloat16)
    down_two[...] = (keep[1] + down[1].astype(wide) + far_rows * (1.0 - to_up)).astype(jnp.bfloat16)


def finish_kernel(own, up, down, last_up, last_down, near, rest):
    wide = jnp.float32
    y_sum = own[...] + up[0].astype(wide) + down[0].astype(wide)
    y_sum = y_sum + last_up[...].astype(wide) + last_down[...].astype(wide)
    rounded = y_sum.astype(jnp.bfloat16)
    near[...] = rounded
    rest[...] = y_sum - rounded.astype(wide)


def activate_kernel(halves, rest, spread_out):
    wide = jnp.float32
    rows, units = spread_out.shape[1:]
    summed = rest[...] + halves[:rows].astype(wide) + halves[rows:].astype(wide)
    gate = summed[:, :units]
    hidden = (gate / (1.0 + jnp.exp(-gate)) * summed[:, units:]).astype(jnp.bfloat16)
    for at in range(spread_out.shape[0]):
        spread_out[at] = hidden


def down_kernel(core, hidden, weight, own, give):
    blocks, rows, units = hidden.shape
    left = hidden[...].reshape(blocks * rows, units)
    half = own.shape[1]
    mine = pl.ds(pl.multiple_of(core[0] * half, half), half)
    other = pl.ds(pl.multiple_of((1 - core[0]) * half, half), half)
    own[...] = jnp.dot(left, weight[:, mine], preferred_element_type=jnp.float32)
    give[...] = jnp.dot(left, weight[:, other], preferred_element_type=jnp.float32).astype(jnp.bfloat16)


def scatter_sum(far, ups, downs, keep, own):
    core = lax.axis_index("c").astype(jnp.int32).reshape(1)
    far = shift_by_core(far, -2)
    up = shift(ups, 1)
    down = shift(downs, -1)
    one = far.shape
    down_two, up_two = small_call(
        merge_kernel,
        ((one, jnp.bfloat16), (one, jnp.bfloat16)),
        core, far, up, down, keep, smem=1,
    )
    last_down = shift(down_two, -2)
    last_up = shift(up_two, 2)
    return small_call(finish_kernel, ((one, jnp.bfloat16), (one, jnp.float32)), own, up, down, last_down, last_up)


def body(tokens, gate_weight, up_weight, down_weight):
    steps, batch, width = tokens.shape
    rows = steps * batch
    local_ff = gate_weight.shape[0]
    flat = tokens.reshape(rows, width)
    near, rest = scatter_sum(*front(flat, gate_weight, up_weight))
    halves = lax.all_gather(near, "zh", axis=0, tiled=True)
    blocks = (8, rows // 8, local_ff)
    (shares,) = small_call(activate_kernel, ((blocks, jnp.bfloat16),), halves, rest)
    core = lax.axis_index("c").astype(jnp.int32)
    shares, core, first = lax.optimization_barrier((shares, core, core == 0))
    hidden = exchange(shares, "y")
    half = width // 2
    own, give = small_call(
        down_kernel,
        (((rows, half), jnp.float32), ((rows, half), jnp.bfloat16)),
        core.reshape(1), hidden, down_weight, smem=1, flops=2 * rows * local_ff * width,
    )
    given = lax.all_gather(give, "c", axis=0)
    chip = own + jnp.where(first, given[1], given[0]).astype(jnp.float32)
    chip = chip.astype(jnp.bfloat16).reshape(16, rows // 16, half)
    out_share = total(exchange(chip, PLANE)).astype(jnp.bfloat16)
    out_half = spread(out_share, PLANE, 16).reshape(rows, half)
    return lax.all_gather(out_half.reshape(steps, batch, half), "c", axis=2, tiled=True)


def solution(mesh):
    fine = Mesh(mesh.devices.reshape(8, 2, 4, 4, 2), ("y", "zh", "zl", "x", "c"))
    gx, gy = ("y", "zh"), ("zl", "x", "c")
    in_specs = (P(None, None, gx), P(gy, gx), P(gy, gx), P(gy, gx))
    return jax.shard_map(body, mesh=fine, in_specs=in_specs, out_specs=P(None, None, gx), check_vma=False)
```
